32 devices in a mesh: band: 16 (over z, x, core), lev: 2 (over y).
Axes of the slice: x: 2, y: 2, z: 4, core: 2. Of those that a mesh axis runs over, the one named last changes fastest.
Arguments:
- air_fourier_coefficients: float32 [4, 16, 1280, 128], P('lev', None, 'band'), may hold values from -6 to 6
- quadrature_factor: float32 [1280], P('band'), may hold values from 0.5 to 1.5
- associated_polynomial_table: bfloat16 [64, 1280, 1280], P('band'), may hold values from -6 to 6
- east_west_harmonic: int32 [64], replicated, may hold values from 0 to 1279, as said below
- boundary_diffusion: float32 [4, 16, 16, 1280], P('lev', None, None, 'band'), may hold values from -0.25 to 0.25
- bulk_transfer_coefficient: float32 [4, 1280], P('lev', 'band'), may hold values from 0.1 to 1
- skin_heat_earlier: float32 [12, 4, 1280, 128], P(None, 'lev', 'band'), may hold values from -6 to 6
- sea_boundary_values: float32 [4, 512, 1440], P('lev', 'band'), may hold values from -6 to 6
- sea_damping_speed: float32 [4, 512, 1440], P('lev', 'band'), may hold values from 0.02 to 2
- sea_coupling_matrix: float32 [4, 4], replicated, may hold values from -1.75 to 1.75
- patch_active_entries: int32 [16], P('band'), may hold values from 8 to 32, as said below
- sea_southern_parallel: int32 [512], P('band'), may hold values from 0 to 1278, as said below
- sea_northern_share: float32 [512], P('band'), may hold values from 0 to 1
- air_paired_cells: int32 [2, 1280], P(None, 'band'), may hold values from 0 to 511, as said below
- air_second_share: float32 [1280], P('band'), may hold values from 0 to 1
Outputs:
- air_coefficients_end: float32 [4, 16, 1280, 128], P('lev', None, 'band')
- sea_values_end: float32 [4, 512, 1440], P('lev', 'band')
- skin_heat_newest: float32 [12, 4, 1280, 128], P(None, 'lev', 'band')
The draws below stay inside these ranges and needn't reach their ends.
Inputs may be any that keep to these rules, and one draw needn't show every extreme that they name: `east_west_harmonic`: Distinct; positions 2 j and 2 j + 1 hold m and 1279 - m for some m below 640; 0 is among them. `patch_active_entries`: the live slots of a tile come first; the last tile is full. For a slot of tile t, sea_southern_parallel and sea_southern_parallel + 1 lie in t * 80 - 8 to (t + 1) * 80 + 7; they do not decrease along a tile's live slots. `air_paired_cells`: for a latitude of band t both taps are live slots of tiles t - 1, t or t + 1, the first one of tile t, and the two differ.
All inputs are finite; a program needn't handle non-finite values.
Results may differ from the reference program's by a relative error of at most 0.014.
Values may be sent and summed in bfloat16 or wider, within the bound.
A program may use at most 64 MiB of HBM per device.

```python
import math
import jax
import jax.numpy as jnp
from jax import lax

PARALLEL_NUMBER = 1280
NDEG = 1280
OLON = 1440
PROGNOSTIC_NUM = 4
LEVS = 16
SUBSTEP_NUMBER = 12
OROWS = 32
MARG = 8
HARMONIC_NUMBER = 64
LAT_DEV = 80
TILES = 16
OSLOTS = 512


def rows_of_tiles(key):
    tile_key = jax.random.fold_in(key, 11)
    count_key, small_key = jax.random.split(tile_key)
    counts = jax.random.randint(count_key, (TILES,), OROWS // 4, OROWS + 1)
    smallest = jax.random.randint(small_key, (), 0, TILES - 1)
    tile_ids = jnp.arange(TILES)
    counts = jnp.where(tile_ids == smallest, OROWS // 4, counts)
    counts = jnp.where(tile_ids == TILES - 1, OROWS, counts)
    return counts.astype(jnp.int32)


def draw_patch_active_entries(key, part):
    return rows_of_tiles(key)


def draw_sea_southern_parallel(key, part):
    counts = rows_of_tiles(key)
    slot_index = jnp.arange(TILES * OROWS, dtype=jnp.int32)
    tile_index = slot_index // OROWS
    within = slot_index % OROWS
    count_here = counts[tile_index]
    within = jnp.minimum(within, count_here - 1)
    span_rows = LAT_DEV + 2 * MARG - 1
    lower = tile_index * LAT_DEV - MARG + within * span_rows // count_here
    lower = jnp.where((tile_index == TILES - 1) & (within == count_here - 1), PARALLEL_NUMBER - 2, lower)
    return jnp.clip(lower, 0, PARALLEL_NUMBER - 2).astype(jnp.int32)


def draw_air_paired_cells(key, part):
    counts = rows_of_tiles(key)
    latitude = jnp.arange(PARALLEL_NUMBER, dtype=jnp.int32)
    band_index = latitude // LAT_DEV
    within = latitude % LAT_DEV
    count_here = counts[band_index]
    first_slot = within * count_here // LAT_DEV
    first_cell_index = band_index * OROWS + first_slot
    next_slot = jnp.where(first_slot + 1 < count_here, first_slot + 1, first_slot - 1)
    before_ok = (within < MARG) & (band_index > 0)
    after_ok = (within >= LAT_DEV - MARG) & (band_index < TILES - 1) & jnp.logical_not(before_ok)
    count_before = counts[jnp.clip(band_index - 1, 0, TILES - 1)]
    closing_cell_index = jnp.where(before_ok, (band_index - 1) * OROWS + count_before - 1, jnp.where(after_ok, (band_index + 1) * OROWS, band_index * OROWS + next_slot))
    return jnp.stack([first_cell_index, closing_cell_index]).astype(jnp.int32)


def draw_east_west_harmonic(key, part):
    wave_key = jax.random.fold_in(key, 23)
    pick_key, order_key = jax.random.split(wave_key)
    half_count = NDEG // 2
    pair_count = HARMONIC_NUMBER // 2
    others = jax.random.permutation(pick_key, half_count - 1)[:pair_count - 1] + 1
    lowest = jnp.concatenate([jnp.zeros((1,), jnp.int32), others.astype(jnp.int32)])
    lowest = lowest[jax.random.permutation(order_key, pair_count)]
    paired = jnp.stack([lowest, NDEG - 1 - lowest], axis=1).reshape(HARMONIC_NUMBER)
    return paired.astype(jnp.int32)


def level_of(key, dims, shards, low, top_value):
    gain, own = 1.0, jax.random.fold_in(key, 6)
    for dim, shards_of in shards:
        steps = jnp.exp(jax.random.uniform(jax.random.fold_in(own, dim), (shards_of,), jnp.float32, low / len(shards), top_value / len(shards)))
        gain = gain * jnp.repeat(steps, dims[dim] // shards_of).reshape([-1 if axis == dim else 1 for axis in range(len(dims))])
    return gain


def gaussian(key, shape, spread, limit, pieces=(), kind=jnp.bfloat16):
    level = level_of(key, shape, pieces, -0.22, 0.18) if pieces else 1.0
    entries = jax.random.normal(key, shape, jnp.float32) * spread * level
    return jnp.minimum(jnp.maximum(entries, -limit), limit).astype(kind)


def setup_inputs(seed: int = 0) -> dict:
    streams_of = jax.random.split(jax.random.key(seed), 16)
    return {
        "air_fourier_coefficients": gaussian(streams_of[0], (PROGNOSTIC_NUM, LEVS, PARALLEL_NUMBER, 2 * HARMONIC_NUMBER), 1.0, 6.0, ((0, 2), (2, 16)), jnp.float32),
        "quadrature_factor": jnp.clip(0.5 + 1.0 * jax.random.uniform(streams_of[1], (PARALLEL_NUMBER,), jnp.float32) ** level_of(streams_of[1], (PARALLEL_NUMBER,), ((0, 16),), -0.2, 0.2), 0.5, 1.5),
        "associated_polynomial_table": gaussian(streams_of[2], (HARMONIC_NUMBER, PARALLEL_NUMBER, NDEG), 1.0, 6.0, ((0, 16),)),
        "east_west_harmonic": draw_east_west_harmonic(jax.random.fold_in(streams_of[15], 71), 0),
        "boundary_diffusion": gaussian(streams_of[4], (PROGNOSTIC_NUM, LEVS, LEVS, PARALLEL_NUMBER), 0.04, 0.25, ((0, 2), (3, 16)), jnp.float32),
        "bulk_transfer_coefficient": jnp.clip(jnp.exp(math.log(1.0) - 2.3025851 * jax.random.uniform(streams_of[5], (PROGNOSTIC_NUM, PARALLEL_NUMBER), jnp.float32) ** level_of(streams_of[5], (PROGNOSTIC_NUM, PARALLEL_NUMBER), ((0, 2), (1, 16)), -0.2, 0.2)), 0.1, 1.0),
        "skin_heat_earlier": gaussian(streams_of[6], (SUBSTEP_NUMBER, PROGNOSTIC_NUM, PARALLEL_NUMBER, 2 * HARMONIC_NUMBER), 1.0, 6.0, ((1, 2), (2, 16)), jnp.float32),
        "sea_boundary_values": gaussian(streams_of[7], (PROGNOSTIC_NUM, OSLOTS, OLON), 1.0, 6.0, ((0, 2), (1, 16)), jnp.float32),
        "sea_damping_speed": jnp.clip(jnp.exp(math.log(2.0) - 4.6051702 * jax.random.uniform(streams_of[8], (PROGNOSTIC_NUM, OSLOTS, OLON), jnp.float32) ** level_of(streams_of[8], (PROGNOSTIC_NUM, OSLOTS, OLON), ((0, 2), (1, 16)), -0.2, 0.2)), 0.02, 2.0),
        "sea_coupling_matrix": gaussian(streams_of[9], (PROGNOSTIC_NUM, PROGNOSTIC_NUM), 0.3, 1.75, (), jnp.float32),
        "patch_active_entries": draw_patch_active_entries(jax.random.fold_in(streams_of[15], 71), 0),
        "sea_southern_parallel": draw_sea_southern_parallel(jax.random.fold_in(streams_of[15], 71), 0),
        "sea_northern_share": jnp.clip(1.0 * jax.random.uniform(streams_of[12], (OSLOTS,), jnp.float32) ** level_of(streams_of[12], (OSLOTS,), ((0, 16),), -0.2, 0.2), 0.0, 1.0),
        "air_paired_cells": draw_air_paired_cells(jax.random.fold_in(streams_of[15], 71), 0),
        "air_second_share": jnp.clip(1.0 * jax.random.uniform(streams_of[14], (PARALLEL_NUMBER,), jnp.float32) ** level_of(streams_of[14], (PARALLEL_NUMBER,), ((0, 16),), -0.2, 0.2), 0.0, 1.0),
    }


degree_damping = 2e-06
ocean_step = 0.5
mixing_diagonal = 0.95
synth_divisor = 4.0

def damping_table(wave_values):
    degrees = wave_values[:, None] + jnp.arange(NDEG, dtype=jnp.int32)[None, :]
    degree_float = degrees.astype(jnp.float32)
    factor = 1.0 / (1.0 + degree_damping * degree_float * (degree_float + 1.0))
    return jnp.where(degrees < NDEG, factor, jnp.zeros_like(factor))

def zonal_table(wave_values):
    longitude = jnp.arange(OLON, dtype=jnp.int32)
    phases = wave_values[:, None] * longitude[None, :] % OLON
    angles = phases.astype(jnp.float32) * (2.0 * math.pi / OLON)
    stacked = jnp.stack([jnp.cos(angles), -jnp.sin(angles)], axis=1)
    return stacked.reshape(2 * wave_values.shape[0], OLON).astype(jnp.bfloat16)

def mixing_matrix(boundary_diffusion):
    level_count = boundary_diffusion.shape[1]
    identity_block = jnp.eye(level_count, dtype=jnp.float32)[None, :, :, None]
    return mixing_diagonal * identity_block + boundary_diffusion - jnp.transpose(boundary_diffusion, (0, 2, 1, 3))

def legendre_pair(inputs):
    values, table, damping = inputs
    spectral = jnp.einsum('rlc,ln->rnc', values.astype(jnp.float32), table.astype(jnp.float32))
    damped = (spectral * damping[None, :, None]).astype(jnp.bfloat16)
    synthesis = jnp.einsum('rnc,ln->rlc', damped.astype(jnp.float32), table.astype(jnp.float32))
    synthesis = synthesis * (1.0 / (synth_divisor * math.sqrt(NDEG)))
    return synthesis.astype(jnp.bfloat16)

def reference(air_fourier_coefficients, quadrature_factor, associated_polynomial_table, east_west_harmonic, boundary_diffusion, bulk_transfer_coefficient, skin_heat_earlier, sea_boundary_values, sea_damping_speed, sea_coupling_matrix, patch_active_entries, sea_southern_parallel, sea_northern_share, air_paired_cells, air_second_share):
    fields = air_fourier_coefficients.shape[0]
    height_pile = air_fourier_coefficients.shape[1]
    row_count = fields * height_pile
    damping = damping_table(east_west_harmonic)
    mixing = mixing_matrix(boundary_diffusion)
    weight = quadrature_factor * (1.0 / math.sqrt(PARALLEL_NUMBER))

    def march_air_model(air_model_present, skin_heat_present):
        scaled = (air_model_present * weight[None, None, :, None]).astype(jnp.bfloat16)
        columns = scaled.reshape(row_count, PARALLEL_NUMBER, HARMONIC_NUMBER, 2).transpose(2, 0, 1, 3)
        synthesis = lax.map(legendre_pair, (columns, associated_polynomial_table, damping))
        synthesis = synthesis.transpose(1, 2, 0, 3).reshape(fields, height_pile, PARALLEL_NUMBER, 2 * HARMONIC_NUMBER).astype(jnp.float32)
        halfway_point = air_model_present - synthesis
        bottom_sheet = bulk_transfer_coefficient[:, :, None] * (skin_heat_present - halfway_point[:, height_pile - 1])
        mixed_state = jnp.einsum('flpa,fpac->flac', mixing, halfway_point, precision=lax.Precision.HIGHEST)
        mixed_state = mixed_state.at[:, height_pile - 1].add(bottom_sheet)
        return (mixed_state, bottom_sheet.astype(jnp.bfloat16))
    air_coefficients_end, forcing_series = lax.scan(march_air_model, air_fourier_coefficients, skin_heat_earlier)
    slot_index = jnp.arange(OSLOTS, dtype=jnp.int32)
    live_slot = slot_index % OROWS < patch_active_entries[slot_index // OROWS]
    low_tap = jnp.where(live_slot, 1.0 - sea_northern_share, jnp.zeros_like(sea_northern_share)).astype(jnp.bfloat16)
    high_tap = jnp.where(live_slot, sea_northern_share, jnp.zeros_like(sea_northern_share)).astype(jnp.bfloat16)
    lower_rows = jnp.take(forcing_series, sea_southern_parallel, axis=2).astype(jnp.float32)
    upper_rows = jnp.take(forcing_series, sea_southern_parallel + 1, axis=2).astype(jnp.float32)
    ocean_flux = (low_tap.astype(jnp.float32)[None, None, :, None] * lower_rows + high_tap.astype(jnp.float32)[None, None, :, None] * upper_rows).astype(jnp.bfloat16)
    zonal_basis = zonal_table(east_west_harmonic).astype(jnp.float32)
    synth_scale = 1.0 / math.sqrt(2 * HARMONIC_NUMBER)
    skew_coupling = sea_coupling_matrix - sea_coupling_matrix.T

    def ocean_advance(ocean_now, flux_now):
        forcing = jnp.einsum('fsc,cx->fsx', flux_now.astype(jnp.float32), zonal_basis) * synth_scale
        coarse = lax.optimization_barrier(ocean_now.astype(jnp.bfloat16)).astype(jnp.float32)
        coupled = jnp.einsum('fe,esx->fsx', skew_coupling, coarse, precision=lax.Precision.HIGHEST)
        updated = (ocean_now + ocean_step * (coupled - forcing)) / (1.0 + ocean_step * sea_damping_speed)
        return (updated, updated.astype(jnp.bfloat16))
    sea_values_end, ocean_wave = lax.scan(ocean_advance, sea_boundary_values, ocean_flux)

    def analyse(wave_now):
        coef = jnp.einsum('fsx,cx->fsc', wave_now.astype(jnp.float32), zonal_basis) * (1.0 / math.sqrt(OLON))
        return coef.astype(jnp.bfloat16)
    ocean_coef = lax.map(analyse, ocean_wave)
    first_cell_index = (1.0 - air_second_share).astype(jnp.bfloat16).astype(jnp.float32)
    closing_cell_index = air_second_share.astype(jnp.bfloat16).astype(jnp.float32)
    first_band_entries = jnp.take(ocean_coef, air_paired_cells[0], axis=2).astype(jnp.float32)
    final_band_entries = jnp.take(ocean_coef, air_paired_cells[1], axis=2).astype(jnp.float32)
    skin_heat_newest = first_cell_index[None, None, :, None] * first_band_entries + closing_cell_index[None, None, :, None] * final_band_entries
    return (air_coefficients_end, sea_values_end, skin_heat_newest)
```

```python
import functools
import math

import jax
import jax.numpy as jnp
from jax import lax
from jax.experimental import pallas as pl
from jax.experimental.pallas import tpu as pltpu
from jax.sharding import PartitionSpec as P

degree_damping = 2e-06
ocean_step = 0.5
mixing_diagonal = 0.95
synth_divisor = 4.0

LANES = 128
WIDE = 256
SUBLANES = 8
VMEM_LIMIT = 52 * 1024 * 1024


def zonal_table(wave_values, lon_count):
    longitude = jnp.arange(lon_count, dtype=jnp.int32)
    phases = wave_values[:, None] * longitude[None, :] % lon_count
    angles = phases.astype(jnp.float32) * (2.0 * math.pi / lon_count)
    stacked = jnp.stack([jnp.cos(angles), -jnp.sin(angles)], axis=1)
    return stacked.reshape(2 * wave_values.shape[0], lon_count).astype(jnp.bfloat16)


def live_tiles(wave_values, degree_count, tile_count):
    live = degree_count - wave_values
    blocks = (live + LANES - 1) // LANES
    ends = jnp.cumsum(blocks)
    tile = jnp.arange(tile_count, dtype=jnp.int32)
    wave = jnp.sum((tile[:, None] >= ends[None, :]).astype(jnp.int32), axis=1)
    wave = jnp.minimum(wave, wave_values.shape[0] - 1)
    one_hot = wave[:, None] == jnp.arange(wave_values.shape[0], dtype=jnp.int32)[None, :]
    start = jnp.sum(jnp.where(one_hot, (ends - blocks)[None, :], 0), axis=1)
    block = jnp.minimum(tile - start, degree_count // LANES - 1)
    owner = jnp.sum(jnp.where(one_hot, wave_values[None, :], 0), axis=1)
    degree = (owner + block * LANES)[:, None] + jnp.arange(LANES, dtype=jnp.int32)[None, :]
    used = (tile < ends[-1])[:, None] & (degree < degree_count)
    degree_float = degree.astype(jnp.float32)
    factor = 1.0 / (1.0 + degree_damping * degree_float * (degree_float + 1.0))
    factor = jnp.where(used, factor, 0.0).reshape(tile_count * LANES)
    column_wave = jnp.repeat(jnp.arange(wave_values.shape[0], dtype=jnp.int32), 2)
    owner_wave = jnp.repeat(wave, LANES)
    damping = jnp.where(column_wave[:, None] == owner_wave[None, :], factor[None, :], 0.0)
    return wave.astype(jnp.int32), block.astype(jnp.int32), damping


def air_kernel(
    dims, wave_ref, block_ref, table_ref, start_ref, skin_ref, skew_ref, bulk_ref, weight_ref,
    damping_ref, end_ref, flux_ref, packed, state, scaled, damped, sem,
):
    fields, levels, columns, steps, tiles = dims
    lat_count = state.shape[1]
    rows = state.shape[0]

    def tile_copy(i):
        return pltpu.make_async_copy(
            table_ref.at[wave_ref[i], :, pl.ds(pl.multiple_of(block_ref[i] * LANES, LANES), LANES)],
            packed.at[:, pl.ds(i * LANES, LANES)],
            sem.at[i],
        )

    for i in range(tiles):
        tile_copy(i).start()
    state[...] = start_ref[...].astype(jnp.float32)
    scaled[...] = (state[...] * weight_ref[...]).astype(jnp.bfloat16)
    for i in range(tiles):
        tile_copy(i).wait()

    def step(k, carry):
        for n in range(0, tiles * LANES, WIDE):
            width = min(WIDE, tiles * LANES - n)
            spectral = jnp.dot(
                scaled[...], packed[:, n : n + width], preferred_element_type=jnp.float32
            )
            factor = damping_ref[:, n : n + width]
            spectral = spectral.reshape(rows // columns, columns, width) * factor[None]
            damped[:, n : n + width] = spectral.reshape(rows, width).astype(jnp.bfloat16)
        for g in range(0, lat_count, WIDE):
            synthesis = lax.dot_general(
                damped[...],
                packed[g : g + WIDE, :],
                (((1,), (1,)), ((), ())),
                preferred_element_type=jnp.float32,
            )
            for h in range(0, WIDE, LANES):
                lanes = slice(g + h, g + h + LANES)
                flux_parts = []
                for f in range(fields):
                    middle = []
                    for l in range(levels):
                        row = (f * levels + l) * columns
                        middle.append(
                            state[row : row + columns, lanes]
                            - synthesis[row : row + columns, h : h + LANES]
                        )
                    heat = skin_ref[k, f * columns : (f + 1) * columns, lanes].astype(jnp.float32)
                    flux = bulk_ref[f : f + 1, lanes] * (heat - middle[levels - 1])
                    flux_parts.append(flux)
                    total = [mixing_diagonal * value for value in middle]
                    total[levels - 1] = total[levels - 1] + flux
                    pair = f * (levels * (levels - 1) // 2)
                    for l in range(levels):
                        for p in range(l + 1, levels):
                            skew = skew_ref[pair : pair + 1, lanes]
                            total[l] = total[l] + skew * middle[p]
                            total[p] = total[p] - skew * middle[l]
                            pair += 1
                    for l in range(levels):
                        row = (f * levels + l) * columns
                        state[row : row + columns, lanes] = total[l]
                flux_ref[k, :, lanes] = jnp.concatenate(flux_parts, axis=0).astype(jnp.bfloat16)
        scaled[...] = (state[...] * weight_ref[...]).astype(jnp.bfloat16)
        return carry

    lax.fori_loop(0, steps, step, 0)
    end_ref[...] = state[...].astype(jnp.bfloat16)


def ocean_kernel(
    dims, skew_ref, ocean_ref, damping_ref, flux_ref, basis_ref, end_ref, coef_ref, state, inverse
):
    fields, rows, steps = dims
    lon_count = ocean_ref.shape[1]
    column_count = basis_ref.shape[0]
    inverse[...] = 1.0 / (1.0 + ocean_step * damping_ref[...])
    state[...] = ocean_ref[...]

    def step(k, carry):
        forcing = jnp.dot(flux_ref[k], basis_ref[...], preferred_element_type=jnp.float32)
        forcing = forcing * (1.0 / math.sqrt(column_count))
        coarse = state[...].astype(jnp.bfloat16).astype(jnp.float32)
        coarse = coarse.reshape(fields, rows, lon_count)
        coupled = []
        for f in range(fields):
            total = skew_ref[f, 0] * coarse[0]
            for e in range(1, fields):
                total = total + skew_ref[f, e] * coarse[e]
            coupled.append(total)
        coupled = jnp.stack(coupled).reshape(fields * rows, lon_count)
        updated = (state[...] + ocean_step * (coupled - forcing)) * inverse[...]
        state[...] = updated
        coef = lax.dot_general(
            updated.astype(jnp.bfloat16),
            basis_ref[...],
            (((1,), (1,)), ((), ())),
            preferred_element_type=jnp.float32,
        )
        coef_ref[k] = (coef * (1.0 / math.sqrt(lon_count))).astype(jnp.bfloat16)
        return carry

    lax.fori_loop(0, steps, step, 0)
    end_ref[...] = state[...]


def vmem():
    return pl.BlockSpec(memory_space=pltpu.VMEM)


def smem():
    return pl.BlockSpec(memory_space=pltpu.SMEM)


def per_device(
    air_fourier_coefficients,
    quadrature_factor,
    associated_polynomial_table,
    east_west_harmonic,
    boundary_diffusion,
    bulk_transfer_coefficient,
    skin_heat_earlier,
    sea_boundary_values,
    sea_damping_speed,
    sea_coupling_matrix,
    patch_active_entries,
    sea_southern_parallel,
    sea_northern_share,
    air_paired_cells,
    air_second_share,
):
    band_index = lax.axis_index("band")
    bands = lax.axis_size("band")
    levs = lax.axis_size("lev")
    fields, levels, lat_local, column_total = air_fourier_coefficients.shape
    steps = skin_heat_earlier.shape[0]
    owned, lat_count, degree_count = associated_polynomial_table.shape
    columns = 2 * owned
    slot_rows = sea_boundary_values.shape[1]
    lon_count = sea_boundary_values.shape[2]
    all_fields = fields * levs
    part_rows = slot_rows // levs
    wave_values = lax.dynamic_slice_in_dim(east_west_harmonic, band_index * owned, owned, 0)
    tiles = (owned // 2) * (degree_count // LANES + 1)

    air_rows = fields * levels
    outgoing = jnp.concatenate(
        [
            air_fourier_coefficients.reshape(air_rows, lat_local, column_total),
            skin_heat_earlier.reshape(steps * fields, lat_local, column_total),
        ]
    ).astype(jnp.bfloat16)
    arrived = lax.all_to_all(
        outgoing.transpose(0, 2, 1), "band", split_axis=1, concat_axis=2, tiled=True
    )
    air_start = arrived[:air_rows].reshape(air_rows * columns, lat_count)
    skin = arrived[air_rows:].reshape(steps, fields * columns, lat_count)

    skew = boundary_diffusion - jnp.transpose(boundary_diffusion, (0, 2, 1, 3))
    skew = jnp.concatenate([skew[:, l, l + 1 :] for l in range(levels - 1)], axis=1)
    skew = skew.reshape(-1, lat_local).astype(jnp.bfloat16)
    skew = lax.all_gather(skew, "band", axis=1, tiled=True).astype(jnp.float32)

    live_slot = jnp.arange(slot_rows, dtype=jnp.int32) < patch_active_entries[0]
    low_tap = jnp.where(live_slot, 1.0 - sea_northern_share, 0.0)
    high_tap = jnp.where(live_slot, sea_northern_share, 0.0)
    small = jnp.concatenate(
        [
            quadrature_factor * (1.0 / math.sqrt(lat_count)),
            bulk_transfer_coefficient.reshape(-1),
            low_tap,
            high_tap,
            sea_southern_parallel.astype(jnp.float32),
        ]
    )
    small = lax.all_gather(small, "band", axis=0, tiled=False)
    near = (1 + fields) * lat_local
    weight = small[:, :lat_local].reshape(1, lat_count)
    bulk = small[:, lat_local:near].reshape(bands, fields, lat_local)
    bulk = bulk.transpose(1, 0, 2).reshape(fields, lat_count)
    low_all = small[:, near : near + slot_rows].reshape(-1).astype(jnp.bfloat16)
    high_all = small[:, near + slot_rows : near + 2 * slot_rows].reshape(-1).astype(jnp.bfloat16)
    lower = small[:, near + 2 * slot_rows :].reshape(-1).astype(jnp.int32)
    latitude = jnp.arange(lat_count, dtype=jnp.int32)[:, None]
    zero = jnp.zeros((), jnp.bfloat16)
    flux_taps = jnp.where(latitude == lower[None, :], low_all[None, :], zero) + jnp.where(
        latitude == lower[None, :] + 1, high_all[None, :], zero
    )

    sea = jnp.stack([sea_boundary_values, sea_damping_speed])
    sea = lax.all_to_all(sea, "lev", split_axis=2, concat_axis=1, tiled=True)
    sea = sea.reshape(2, all_fields * part_rows, lon_count)

    tile_wave, tile_block, damping = live_tiles(wave_values, degree_count, tiles)
    damping = damping * (1.0 / (synth_divisor * math.sqrt(degree_count)))
    rows = air_rows * columns
    air_end, flux = pl.pallas_call(
        functools.partial(air_kernel, (fields, levels, columns, steps, tiles)),
        out_shape=(
            jax.ShapeDtypeStruct((rows, lat_count), jnp.bfloat16),
            jax.ShapeDtypeStruct((steps, fields * columns, lat_count), jnp.bfloat16),
        ),
        in_specs=[smem(), smem(), pl.BlockSpec(memory_space=pl.ANY)] + [vmem()] * 6,
        out_specs=(vmem(), vmem()),
        scratch_shapes=[
            pltpu.VMEM((lat_count, tiles * LANES), jnp.bfloat16),
            pltpu.VMEM((rows, lat_count), jnp.float32),
            pltpu.VMEM((rows, lat_count), jnp.bfloat16),
            pltpu.VMEM((rows, tiles * LANES), jnp.bfloat16),
            pltpu.SemaphoreType.DMA((tiles,)),
        ],
        compiler_params=pltpu.CompilerParams(vmem_limit_bytes=VMEM_LIMIT),
        cost_estimate=pl.CostEstimate(
            flops=4 * steps * rows * lat_count * tiles * LANES,
            bytes_accessed=2 * lat_count * tiles * LANES,
            transcendentals=0,
        ),
        name="air_march",
    )(
        tile_wave, tile_block, associated_polynomial_table, air_start, skin, skew, bulk, weight,
        damping,
    )

    returned = lax.all_to_all(
        air_end.reshape(air_rows, columns, lat_count), "band", split_axis=2, concat_axis=1, tiled=True
    )
    air_coefficients_end = (
        returned.transpose(0, 2, 1)
        .reshape(fields, levels, lat_local, column_total)
        .astype(jnp.float32)
    )

    ocean_flux = jnp.dot(
        flux.reshape(steps * fields * columns, lat_count),
        flux_taps,
        preferred_element_type=jnp.float32,
    ).astype(jnp.bfloat16)
    ocean_flux = ocean_flux.reshape(steps, fields, columns, bands * levs, part_rows)
    ocean_flux = ocean_flux.transpose(3, 0, 1, 4, 2)
    ocean_flux = lax.all_to_all(
        ocean_flux, ("band", "lev"), split_axis=0, concat_axis=0, tiled=True
    )
    ocean_flux = ocean_flux.reshape(bands, levs, steps, fields, part_rows, columns)
    ocean_flux = ocean_flux.transpose(2, 1, 3, 4, 0, 5)
    ocean_flux = ocean_flux.reshape(steps, all_fields * part_rows, column_total)

    zonal_basis = zonal_table(east_west_harmonic, lon_count)
    skew_full = sea_coupling_matrix - sea_coupling_matrix.T
    sea_rows = all_fields * part_rows
    sea_end, ocean_coef = pl.pallas_call(
        functools.partial(ocean_kernel, (all_fields, part_rows, steps)),
        out_shape=(
            jax.ShapeDtypeStruct((sea_rows, lon_count), jnp.float32),
            jax.ShapeDtypeStruct((steps, sea_rows, column_total), jnp.bfloat16),
        ),
        in_specs=[smem()] + [vmem()] * 4,
        out_specs=(vmem(), vmem()),
        scratch_shapes=[pltpu.VMEM((sea_rows, lon_count), jnp.float32)] * 2,
        compiler_params=pltpu.CompilerParams(vmem_limit_bytes=VMEM_LIMIT),
        cost_estimate=pl.CostEstimate(
            flops=4 * steps * sea_rows * lon_count * column_total,
            bytes_accessed=12 * sea_rows * lon_count,
            transcendentals=0,
        ),
        name="ocean_march",
    )(skew_full, sea[0], sea[1], ocean_flux, zonal_basis)

    sea_values_end = lax.all_to_all(
        sea_end.reshape(all_fields, part_rows, lon_count), "lev", split_axis=0, concat_axis=1, tiled=True
    )
    ocean_coef = ocean_coef.reshape(steps, all_fields, part_rows, column_total)
    ocean_coef = lax.all_to_all(ocean_coef, "lev", split_axis=1, concat_axis=2, tiled=True)
    up = [(i, i + 1) for i in range(bands - 1)]
    down = [(j, i) for i, j in up]
    before = lax.ppermute(ocean_coef, "band", up)
    after = lax.ppermute(ocean_coef, "band", down)
    neighbours = jnp.concatenate([before, ocean_coef, after], axis=2)
    base_slot = (band_index - 1) * slot_rows
    slot_index = jnp.arange(3 * slot_rows, dtype=jnp.int32)[None, :]
    first_local = (air_paired_cells[0] - base_slot)[:, None]
    second_local = (air_paired_cells[1] - base_slot)[:, None]
    return_taps = jnp.where(
        slot_index == first_local, (1.0 - air_second_share)[:, None], 0.0
    ) + jnp.where(slot_index == second_local, air_second_share[:, None], 0.0)
    return_taps = return_taps.astype(jnp.bfloat16)
    skin_heat_newest = jnp.einsum(
        "ga,kfac->kfgc", return_taps, neighbours, preferred_element_type=jnp.float32
    )
    return (air_coefficients_end, sea_values_end, skin_heat_newest)


def solution(mesh):
    return jax.shard_map(
        per_device,
        mesh=mesh,
        in_specs=(
            P("lev", None, "band", None),
            P("band"),
            P("band", None, None),
            P(),
            P("lev", None, None, "band"),
            P("lev", "band"),
            P(None, "lev", "band", None),
            P("lev", "band", None),
            P("lev", "band", None),
            P(),
            P("band"),
            P("band"),
            P("band"),
            P(None, "band"),
            P("band"),
        ),
        out_specs=(
            P("lev", None, "band", None),
            P("lev", "band", None),
            P(None, "lev", "band", None),
        ),
        check_vma=False,
    )
```

```python
import functools
import math

import jax
import jax.numpy as jnp
from jax import lax
from jax.experimental import pallas as pl
from jax.experimental.pallas import tpu as pltpu
from jax.sharding import PartitionSpec as P

degree_damping = 2e-06
ocean_step = 0.5
mixing_diagonal = 0.95
synth_divisor = 4.0

LANES = 128
WIDE = 256
SUBLANES = 8
VMEM_LIMIT = 52 * 1024 * 1024


def zonal_table(wave_values, lon_count):
    longitude = jnp.arange(lon_count, dtype=jnp.int32)
    phases = wave_values[:, None] * longitude[None, :] % lon_count
    angles = phases.astype(jnp.float32) * (2.0 * math.pi / lon_count)
    stacked = jnp.stack([jnp.cos(angles), -jnp.sin(angles)], axis=1)
    return stacked.reshape(2 * wave_values.shape[0], lon_count).astype(jnp.bfloat16)


def live_tiles(wave_values, degree_count, tile_count):
    live = degree_count - wave_values
    blocks = (live + LANES - 1) // LANES
    ends = jnp.cumsum(blocks)
    tile = jnp.arange(tile_count, dtype=jnp.int32)
    wave = jnp.sum((tile[:, None] >= ends[None, :]).astype(jnp.int32), axis=1)
    wave = jnp.minimum(wave, wave_values.shape[0] - 1)
    one_hot = wave[:, None] == jnp.arange(wave_values.shape[0], dtype=jnp.int32)[None, :]
    start = jnp.sum(jnp.where(one_hot, (ends - blocks)[None, :], 0), axis=1)
    block = jnp.minimum(tile - start, degree_count // LANES - 1)
    owner = jnp.sum(jnp.where(one_hot, wave_values[None, :], 0), axis=1)
    degree = (owner + block * LANES)[:, None] + jnp.arange(LANES, dtype=jnp.int32)[None, :]
    used = (tile < ends[-1])[:, None] & (degree < degree_count)
    degree_float = degree.astype(jnp.float32)
    factor = 1.0 / (1.0 + degree_damping * degree_float * (degree_float + 1.0))
    factor = jnp.where(used, factor, 0.0).reshape(tile_count * LANES)
    column_wave = jnp.repeat(jnp.arange(wave_values.shape[0], dtype=jnp.int32), 2)
    owner_wave = jnp.repeat(wave, LANES)
    damping = jnp.where(column_wave[:, None] == owner_wave[None, :], factor[None, :], 0.0)
    return wave.astype(jnp.int32), block.astype(jnp.int32), damping


def regroup(read, group, sources, width):
    lane_block = None
    total = None
    offset = group * width
    tile = pl.ds(pl.multiple_of(offset // LANES * LANES, LANES), LANES)
    for place, source in enumerate(sources):
        piece = read(source, tile).astype(jnp.float32)
        shift = lax.rem(place * width - lax.rem(offset, LANES) + LANES, LANES)
        piece = pltpu.roll(piece, shift, 1)
        if total is None:
            lane_block = lax.broadcasted_iota(jnp.int32, piece.shape, 1) // width
            total = jnp.where(lane_block == place, piece, 0.0)
        else:
            total = jnp.where(lane_block == place, piece, total)
    return total


def pack_kernel(columns, air_ref, skin_ref, out_ref):
    air_rows = air_ref.shape[0]
    used = air_rows + skin_ref.shape[0]
    per_tile = LANES // columns

    def read(row, tile):
        return air_ref[row, :, tile] if row < air_rows else skin_ref[row - air_rows, :, tile]

    def one(band, carry):
        for t in range(out_ref.shape[2] // LANES):
            sources = range(t * per_tile, min((t + 1) * per_tile, used))
            out_ref[band, :, t * LANES : (t + 1) * LANES] = regroup(
                read, band, sources, columns
            ).astype(out_ref.dtype)
        return carry

    lax.fori_loop(0, out_ref.shape[0], one, 0)


def unpack_kernel(columns, in_ref, out_ref):
    per_tile = LANES // columns

    def one(row, carry):
        for t in range(out_ref.shape[2] // LANES):
            out_ref[row, :, t * LANES : (t + 1) * LANES] = regroup(
                lambda band, tile: in_ref[band, :, tile],
                row,
                range(t * per_tile, (t + 1) * per_tile),
                columns,
            )
        return carry

    lax.fori_loop(0, out_ref.shape[0], one, 0)


def air_kernel(
    dims, wave_ref, block_ref, table_ref, start_ref, skew_ref, bulk_ref, weight_ref,
    damping_ref, end_ref, flux_ref, packed, state, scaled, damped, sem,
):
    fields, levels, columns, steps, tiles = dims
    lat_count = state.shape[1]
    rows = fields * levels * columns

    def tile_copy(i):
        return pltpu.make_async_copy(
            table_ref.at[wave_ref[i], :, pl.ds(pl.multiple_of(block_ref[i] * LANES, LANES), LANES)],
            packed.at[:, pl.ds(i * LANES, LANES)],
            sem.at[i],
        )

    for i in range(tiles):
        tile_copy(i).start()
    for g in range(0, lat_count, LANES):
        for r in range(0, state.shape[0], LANES):
            block = start_ref[g : g + LANES, r : r + LANES].astype(jnp.float32)
            state[r : r + LANES, g : g + LANES] = block.T
    scaled[...] = (state[:rows] * weight_ref[...]).astype(jnp.bfloat16)
    for i in range(tiles):
        tile_copy(i).wait()

    def step(k, carry):
        for n in range(0, tiles * LANES, WIDE):
            width = min(WIDE, tiles * LANES - n)
            spectral = jnp.dot(
                scaled[...], packed[:, n : n + width], preferred_element_type=jnp.float32
            )
            factor = damping_ref[:, n : n + width]
            spectral = spectral.reshape(rows // columns, columns, width) * factor[None]
            damped[:, n : n + width] = spectral.reshape(rows, width).astype(jnp.bfloat16)
        for g in range(0, lat_count, WIDE):
            synthesis = lax.dot_general(
                damped[...],
                packed[g : g + WIDE, :],
                (((1,), (1,)), ((), ())),
                preferred_element_type=jnp.float32,
            )
            for h in range(0, WIDE, LANES):
                lanes = slice(g + h, g + h + LANES)
                flux_parts = []
                for f in range(fields):
                    middle = []
                    for l in range(levels):
                        row = (f * levels + l) * columns
                        middle.append(
                            state[row : row + columns, lanes]
                            - synthesis[row : row + columns, h : h + LANES]
                        )
                    heat_row = rows + k * (fields * columns) + f * columns
                    heat = state[pl.ds(pl.multiple_of(heat_row, columns), columns), lanes]
                    flux = bulk_ref[f : f + 1, lanes] * (heat - middle[levels - 1])
                    flux_parts.append(flux)
                    total = [mixing_diagonal * value for value in middle]
                    total[levels - 1] = total[levels - 1] + flux
                    pair = f * (levels * (levels - 1) // 2)
                    for l in range(levels):
                        for p in range(l + 1, levels):
                            skew = skew_ref[pair : pair + 1, lanes]
                            total[l] = total[l] + skew * middle[p]
                            total[p] = total[p] - skew * middle[l]
                            pair += 1
                    for l in range(levels):
                        row = (f * levels + l) * columns
                        state[row : row + columns, lanes] = total[l]
                flux_ref[k, :, lanes] = jnp.concatenate(flux_parts, axis=0).astype(jnp.bfloat16)
        scaled[...] = (state[:rows] * weight_ref[...]).astype(jnp.bfloat16)
        return carry

    lax.fori_loop(0, steps, step, 0)
    for g in range(0, lat_count, LANES):
        for r in range(0, rows, LANES):
            block = state[r : r + LANES, g : g + LANES]
            end_ref[g : g + LANES, r : r + LANES] = block.T.astype(jnp.bfloat16)


def ocean_kernel(
    dims, skew_ref, ocean_ref, damping_ref, flux_ref, basis_ref, end_ref, coef_ref, state, inverse,
    flux_now,
):
    fields, own_fields, rows, steps, columns = dims
    per_tile = LANES // columns
    lon_count = ocean_ref.shape[1]
    column_count = basis_ref.shape[0]
    inverse[...] = 1.0 / (1.0 + ocean_step * damping_ref[...])
    state[...] = ocean_ref[...]

    def step(k, carry):
        for f in range(own_fields):
            for t in range(column_count // LANES):
                part = regroup(
                    lambda band, tile: flux_ref[band, :, tile],
                    k * own_fields + f,
                    range(t * per_tile, (t + 1) * per_tile),
                    columns,
                )
                for v in range(fields // own_fields):
                    start = (v * own_fields + f) * rows
                    flux_now[start : start + rows, t * LANES : (t + 1) * LANES] = part[
                        v * rows : (v + 1) * rows
                    ]
        forcing = jnp.dot(
            flux_now[...].astype(jnp.bfloat16), basis_ref[...], preferred_element_type=jnp.float32
        )
        forcing = forcing * (1.0 / math.sqrt(column_count))
        coarse = state[...].astype(jnp.bfloat16).astype(jnp.float32)
        coarse = coarse.reshape(fields, rows, lon_count)
        coupled = []
        for f in range(fields):
            total = skew_ref[f, 0] * coarse[0]
            for e in range(1, fields):
                total = total + skew_ref[f, e] * coarse[e]
            coupled.append(total)
        coupled = jnp.stack(coupled).reshape(fields * rows, lon_count)
        updated = (state[...] + ocean_step * (coupled - forcing)) * inverse[...]
        state[...] = updated
        coef = lax.dot_general(
            updated.astype(jnp.bfloat16),
            basis_ref[...],
            (((1,), (1,)), ((), ())),
            preferred_element_type=jnp.float32,
        )
        coef_ref[k] = (coef * (1.0 / math.sqrt(lon_count))).astype(jnp.bfloat16)
        return carry

    lax.fori_loop(0, steps, step, 0)
    end_ref[...] = state[...]


def vmem():
    return pl.BlockSpec(memory_space=pltpu.VMEM)


def smem():
    return pl.BlockSpec(memory_space=pltpu.SMEM)


def lev_exchange(values, split_axis, concat_axis):
    count = lax.axis_size("lev")
    me = lax.axis_index("lev")
    size = values.shape[split_axis] // count
    pieces = []
    for shift in range(count):
        target = lax.rem(me + shift, count)
        chunk = lax.dynamic_slice_in_dim(values, target * size, size, split_axis)
        if shift:
            chunk = lax.ppermute(chunk, "lev", [(i, (i + shift) % count) for i in range(count)])
        pieces.append(chunk)
    ordered = []
    for source in range(count):
        found = pieces[0]
        for shift in range(1, count):
            found = jnp.where(lax.rem(me - source + count, count) == shift, pieces[shift], found)
        ordered.append(found)
    return jnp.concatenate(ordered, axis=concat_axis)


def per_device(
    air_fourier_coefficients,
    quadrature_factor,
    associated_polynomial_table,
    east_west_harmonic,
    boundary_diffusion,
    bulk_transfer_coefficient,
    skin_heat_earlier,
    sea_boundary_values,
    sea_damping_speed,
    sea_coupling_matrix,
    patch_active_entries,
    sea_southern_parallel,
    sea_northern_share,
    air_paired_cells,
    air_second_share,
):
    band_index = lax.axis_index("band")
    bands = lax.axis_size("band")
    levs = lax.axis_size("lev")
    fields, levels, lat_local, column_total = air_fourier_coefficients.shape
    steps = skin_heat_earlier.shape[0]
    owned, lat_count, degree_count = associated_polynomial_table.shape
    columns = 2 * owned
    slot_rows = sea_boundary_values.shape[1]
    lon_count = sea_boundary_values.shape[2]
    all_fields = fields * levs
    part_rows = slot_rows // levs
    wave_values = lax.dynamic_slice_in_dim(east_west_harmonic, band_index * owned, owned, 0)
    tiles = (owned // 2) * (degree_count // LANES + 1)

    air_rows = fields * levels
    sent_lanes = -(-(air_rows + steps * fields) * columns // LANES) * LANES
    outgoing = pl.pallas_call(
        functools.partial(pack_kernel, columns),
        out_shape=jax.ShapeDtypeStruct((bands, lat_local, sent_lanes), jnp.bfloat16),
        in_specs=[vmem()] * 2,
        out_specs=vmem(),
        compiler_params=pltpu.CompilerParams(vmem_limit_bytes=VMEM_LIMIT),
        name="pack_rows",
    )(
        air_fourier_coefficients.reshape(air_rows, lat_local, column_total),
        skin_heat_earlier.reshape(steps * fields, lat_local, column_total),
    )
    arrived = lax.all_to_all(outgoing, "band", split_axis=0, concat_axis=0, tiled=True)
    air_start = arrived.reshape(lat_count, sent_lanes)

    skew = boundary_diffusion - jnp.transpose(boundary_diffusion, (0, 2, 1, 3))
    skew = jnp.concatenate([skew[:, l, l + 1 :] for l in range(levels - 1)], axis=1)
    skew = skew.reshape(-1, lat_local).astype(jnp.bfloat16)
    pairs = skew.shape[0]

    live_slot = jnp.arange(slot_rows, dtype=jnp.int32) < patch_active_entries[0]
    low_tap = jnp.where(live_slot, 1.0 - sea_northern_share, 0.0)
    high_tap = jnp.where(live_slot, sea_northern_share, 0.0)
    near = (sea_southern_parallel - band_index * lat_local).astype(jnp.float32)
    taps = jnp.concatenate([low_tap, high_tap, near])
    tap_rows = -(-taps.shape[0] // lat_local)
    taps = jnp.pad(taps, (0, tap_rows * lat_local - taps.shape[0])).reshape(tap_rows, lat_local)
    factors = jnp.concatenate(
        [quadrature_factor[None] * (1.0 / math.sqrt(lat_count)), bulk_transfer_coefficient]
    )
    rounded = lax.reduce_precision(factors, exponent_bits=8, mantissa_bits=7)
    small = jnp.concatenate(
        [skew]
        + [value.astype(jnp.bfloat16) for value in (rounded, factors - rounded, taps)]
    )
    small = lax.all_gather(small, "band", axis=0, tiled=False)
    by_row = small[:, : pairs + 2 * (1 + fields)].transpose(1, 0, 2).reshape(-1, lat_count)
    by_row = by_row.astype(jnp.float32)
    skew = by_row[:pairs]
    factors = by_row[pairs : pairs + 1 + fields] + by_row[pairs + 1 + fields :]
    weight = factors[:1]
    bulk = factors[1:]
    taps = small[:, pairs + 2 * (1 + fields) :].reshape(bands, tap_rows * lat_local)
    low_all = taps[:, :slot_rows].reshape(-1)
    high_all = taps[:, slot_rows : 2 * slot_rows].reshape(-1)
    lower = taps[:, 2 * slot_rows : 3 * slot_rows].astype(jnp.int32)
    lower = (lower + lat_local * jnp.arange(bands, dtype=jnp.int32)[:, None]).reshape(-1)
    latitude = jnp.arange(lat_count, dtype=jnp.int32)[None, :]
    zero = jnp.zeros((), jnp.bfloat16)
    flux_taps = jnp.where(latitude == lower[:, None], low_all[:, None], zero) + jnp.where(
        latitude == lower[:, None] + 1, high_all[:, None], zero
    )

    sea = jnp.stack([sea_boundary_values, sea_damping_speed])
    sea = lev_exchange(sea, 2, 1).reshape(2, all_fields * part_rows, lon_count)

    tile_wave, tile_block, damping = live_tiles(wave_values, degree_count, tiles)
    damping = damping * (1.0 / (synth_divisor * math.sqrt(degree_count)))
    rows = air_rows * columns
    air_end, flux = pl.pallas_call(
        functools.partial(air_kernel, (fields, levels, columns, steps, tiles)),
        out_shape=(
            jax.ShapeDtypeStruct((lat_count, rows), jnp.bfloat16),
            jax.ShapeDtypeStruct((steps, fields * columns, lat_count), jnp.bfloat16),
        ),
        in_specs=[smem(), smem(), pl.BlockSpec(memory_space=pl.ANY)] + [vmem()] * 5,
        out_specs=(vmem(), vmem()),
        scratch_shapes=[
            pltpu.VMEM((lat_count, tiles * LANES), jnp.bfloat16),
            pltpu.VMEM((sent_lanes, lat_count), jnp.float32),
            pltpu.VMEM((rows, lat_count), jnp.bfloat16),
            pltpu.VMEM((rows, tiles * LANES), jnp.bfloat16),
            pltpu.SemaphoreType.DMA((tiles,)),
        ],
        compiler_params=pltpu.CompilerParams(vmem_limit_bytes=VMEM_LIMIT),
        cost_estimate=pl.CostEstimate(
            flops=4 * steps * rows * lat_count * tiles * LANES,
            bytes_accessed=2 * lat_count * tiles * LANES,
            transcendentals=0,
        ),
        name="air_march",
    )(
        tile_wave, tile_block, associated_polynomial_table, air_start, skew, bulk, weight,
        damping,
    )

    ocean_flux = lax.dot_general(
        flux_taps,
        flux.reshape(steps * fields * columns, lat_count),
        (((1,), (1,)), ((), ())),
        preferred_element_type=jnp.float32,
    ).astype(jnp.bfloat16)
    flux_lanes = -(-ocean_flux.shape[1] // LANES) * LANES
    ocean_flux = jnp.pad(ocean_flux, ((0, 0), (0, flux_lanes - ocean_flux.shape[1])))
    ocean_flux = lax.all_to_all(
        ocean_flux.reshape(bands * levs, part_rows, flux_lanes),
        ("band", "lev"),
        split_axis=0,
        concat_axis=0,
        tiled=True,
    )
    ocean_flux = ocean_flux.reshape(bands, levs * part_rows, flux_lanes)

    returned = lax.all_to_all(
        air_end.reshape(bands, lat_local, rows), "band", split_axis=0, concat_axis=0, tiled=True
    )
    air_coefficients_end = pl.pallas_call(
        functools.partial(unpack_kernel, columns),
        out_shape=jax.ShapeDtypeStruct((air_rows, lat_local, column_total), jnp.float32),
        in_specs=[vmem()],
        out_specs=vmem(),
        compiler_params=pltpu.CompilerParams(vmem_limit_bytes=VMEM_LIMIT),
        name="unpack_rows",
    )(returned).reshape(air_fourier_coefficients.shape)

    zonal_basis = zonal_table(east_west_harmonic, lon_count)
    skew_full = sea_coupling_matrix - sea_coupling_matrix.T
    sea_rows = all_fields * part_rows
    sea_end, ocean_coef = pl.pallas_call(
        functools.partial(ocean_kernel, (all_fields, fields, part_rows, steps, columns)),
        out_shape=(
            jax.ShapeDtypeStruct((sea_rows, lon_count), jnp.float32),
            jax.ShapeDtypeStruct((steps, sea_rows, column_total), jnp.bfloat16),
        ),
        in_specs=[smem()] + [vmem()] * 4,
        out_specs=(vmem(), vmem()),
        scratch_shapes=[pltpu.VMEM((sea_rows, lon_count), jnp.float32)] * 2
        + [pltpu.VMEM((sea_rows, column_total), jnp.float32)],
        compiler_params=pltpu.CompilerParams(vmem_limit_bytes=VMEM_LIMIT),
        cost_estimate=pl.CostEstimate(
            flops=4 * steps * sea_rows * lon_count * column_total,
            bytes_accessed=12 * sea_rows * lon_count,
            transcendentals=0,
        ),
        name="ocean_march",
    )(skew_full, sea[0], sea[1], ocean_flux, zonal_basis)

    sea_values_end = lev_exchange(
        sea_end.reshape(all_fields, part_rows, lon_count), 0, 1
    )
    lev_index = lax.axis_index("lev")
    ocean_coef = ocean_coef.reshape(steps, all_fields, part_rows, column_total)
    pieces, slots = [], []
    for shift in range(levs):
        chunk = lax.dynamic_slice_in_dim(
            ocean_coef, lax.rem(lev_index + shift, levs) * fields, fields, 1
        )
        source = lax.rem(lev_index - shift + levs, levs)
        for hop in (-1, 0, 1):
            if hop or shift:
                pairs_of = [
                    (b * levs + v, (b + hop) * levs + (v + shift) % levs)
                    for b in range(bands)
                    for v in range(levs)
                    if 0 <= b + hop < bands
                ]
                pieces.append(lax.ppermute(chunk, ("band", "lev"), pairs_of))
            else:
                pieces.append(chunk)
            slots.append((band_index - hop) * slot_rows + source * part_rows)
    neighbours = jnp.concatenate(pieces, axis=2)
    part = jnp.arange(part_rows, dtype=jnp.int32)
    slot_index = jnp.concatenate([slot + part for slot in slots])[None, :]
    first_local = air_paired_cells[0][:, None]
    second_local = air_paired_cells[1][:, None]
    return_taps = jnp.where(
        slot_index == first_local, (1.0 - air_second_share)[:, None], 0.0
    ) + jnp.where(slot_index == second_local, air_second_share[:, None], 0.0)
    return_taps = return_taps.astype(jnp.bfloat16)
    skin_heat_newest = jnp.einsum(
        "ga,kfac->kfgc", return_taps, neighbours, preferred_element_type=jnp.float32
    )
    return (air_coefficients_end, sea_values_end, skin_heat_newest)


def solution(mesh):
    return jax.shard_map(
        per_device,
        mesh=mesh,
        in_specs=(
            P("lev", None, "band", None),
            P("band"),
            P("band", None, None),
            P(),
            P("lev", None, None, "band"),
            P("lev", "band"),
            P(None, "lev", "band", None),
            P("lev", "band", None),
            P("lev", "band", None),
            P(),
            P("band"),
            P("band"),
            P("band"),
            P(None, "band"),
            P("band"),
        ),
        out_specs=(
            P("lev", None, "band", None),
            P("lev", "band", None),
            P(None, "lev", "band", None),
        ),
        check_vma=False,
    )
```
